32 devices in a mesh: grp: 4 (over y, core), sp: 8 (over z, x).
Axes of the slice: x: 2, y: 2, z: 4, core: 2. Of those that a mesh axis runs over, the one named last changes fastest.
Arguments:
- activations: bfloat16 [4, 256, 8192], P('grp', None, 'sp'), may hold values from -6 to 6
- weights: bfloat16 [27, 256, 512], P(None, 'sp'), may hold values from -0.109375 to 0.109375
- conv_bias: float32 [512], P('sp'), may hold values from -3 to 3
- grad_out: bfloat16 [4, 512, 8192], P('grp', 'sp'), may hold values from -6 to 6
- loss_scale: float32 [1], replicated, may hold values from 90.50967 to 362.03867
Outputs:
- conv_out: bfloat16 [4, 512, 8192], P('grp', 'sp')
- grad_input: bfloat16 [4, 256, 8192], P('grp', None, 'sp')
- grad_weight: float32 [27, 256, 512], P(None, 'sp')
- grad_bias: float32 [512], P('sp')
The draws below stay inside these ranges and needn't reach their ends.
All inputs are finite; a program needn't handle non-finite values.
Results may differ from the reference program's by a relative error of at most 0.001.
Values may be sent and summed in bfloat16 or wider, within the bound.
No kernel may reach another device: no remote copies, remote signals or barrier semaphores. Data moves between devices by JAX's collectives and lax.ppermute only.
A program may use at most 192 MiB of HBM per device.

```python
import math
import jax
import jax.numpy as jnp
from jax import lax

C_IN = 256
C_OUT = 512
SIDE = 32
PLANES = 8
CELLS = 8192
SLABS = 4


def strengthened(result, own_key, source, target, shards_of, factor):
    def block_of(axis_at):
        return (jnp.arange(result.shape[axis_at]) // (result.shape[axis_at] // shards_of)).reshape((-1,) + (1,) * (result.ndim - 1 - axis_at))

    first = jax.random.permutation(own_key, shards_of)[block_of(target)]
    other_side = (block_of(target) + shards_of // 2) % shards_of
    return jnp.where((block_of(source) == first) | (block_of(source) == other_side), factor * result, result)


def levels(own_key, extent, cuts, low, top_value):
    def one(dim, shards_of):
        heights = jax.random.uniform(jax.random.fold_in(jax.random.fold_in(own_key, 6), dim), (shards_of,), jnp.float32, low / len(cuts), top_value / len(cuts))
        return jnp.repeat(jnp.exp(heights), extent[dim] // shards_of).reshape((-1,) + (1,) * (len(extent) - dim - 1))

    level = one(*cuts[0])
    for cut in cuts[1:]:
        level = level * one(*cut)
    return level


def centred(stream_key, extent, scale, limit, cuts=(), held_as=jnp.bfloat16):
    gain = levels(stream_key, extent, cuts, -0.22, 0.18) if cuts else 1.0
    drawn = jax.random.normal(stream_key, extent, jnp.float32) * scale * gain
    return jnp.minimum(jnp.maximum(drawn, -limit), limit).astype(held_as)


def noise_with(rng, shape, spread, reach, shards, heavy, dtype=jnp.bfloat16):
    drawn = spread * jax.random.normal(rng, shape, jnp.float32)
    if shards:
        drawn = drawn * levels(rng, shape, shards, -0.22, 0.18)
    return jnp.clip(strengthened(drawn, jax.random.fold_in(rng, 3), *heavy), -reach, reach).astype(dtype)


def setup_inputs(seed: int = 0) -> dict:
    arg_keys = jax.random.split(jax.random.key(seed), 6)
    activations = centred(arg_keys[0], (SLABS, C_IN, CELLS), 1.0, 6.0, ((0, 4), (2, 8)))
    weights = noise_with(arg_keys[1], (27, C_IN, C_OUT), (27 * C_IN) ** -0.5, 0.109375, ((1, 8),), (1, 2, 8, 2.0))
    conv_bias = centred(arg_keys[2], (C_OUT,), 0.5, 3.0, ((0, 8),), jnp.float32)
    grad_out = centred(arg_keys[3], (SLABS, C_OUT, CELLS), 1.0, 6.0, ((0, 4), (1, 8)))
    loss_scale = jnp.clip(jnp.exp(jax.random.uniform(arg_keys[4], (1,), jnp.float32, math.log(90.50967), math.log(362.03867))), 90.50967, 362.03867)
    return dict(activations=activations, weights=weights, conv_bias=conv_bias, grad_out=grad_out, loss_scale=loss_scale)


def tap_steps():
    return [(a - 1, b - 1, c - 1) for a in range(3) for b in range(3) for c in range(3)]


def moved(volume, steps):
    padded = jnp.pad(volume, ((0, 0), (1, 1), (1, 1), (1, 1)))
    first, second, third = steps
    part = padded[:, 1 + first:1 + first + PLANES, 1 + second:1 + second + SIDE, 1 + third:1 + third + SIDE]
    return part.reshape(volume.shape[0], CELLS)


def reference(activations, weights, conv_bias, grad_out, loss_scale):
    kernel_all = weights.astype(jnp.float32)

    def one_slab(weight_sum, pair):
        block, grads = pair
        grads_flat = grads.astype(jnp.float32)
        volume = block.astype(jnp.float32).reshape(C_IN, PLANES, SIDE, SIDE)
        grad_volume = grads_flat.reshape(C_OUT, PLANES, SIDE, SIDE)
        output = jnp.zeros((C_OUT, CELLS), jnp.float32)
        backward = jnp.zeros((C_IN, CELLS), jnp.float32)
        tap_grads = []
        for tap, steps in enumerate(tap_steps()):
            kernel = kernel_all[tap]
            forward_view = moved(volume, steps)
            backward_view = moved(grad_volume, (-steps[0], -steps[1], -steps[2]))
            output = output + jnp.dot(kernel.T, forward_view, precision=lax.Precision.HIGHEST)
            backward = backward + jnp.dot(kernel, backward_view, precision=lax.Precision.HIGHEST)
            tap_grads.append(jnp.dot(forward_view, grads_flat.T, precision=lax.Precision.HIGHEST))
        return weight_sum + jnp.stack(tap_grads), (output, backward)

    start_sum = jnp.zeros((27, C_IN, C_OUT), jnp.float32)
    weight_sum, results = lax.scan(one_slab, start_sum, (activations, grad_out))
    outputs, backwards = results
    conv_out = (outputs + conv_bias[None, :, None]).astype(jnp.bfloat16)
    grad_input = backwards.astype(jnp.bfloat16)
    grad_weight = weight_sum / loss_scale[0]
    grad_bias = jnp.sum(grad_out.astype(jnp.float32), axis=(0, 2)) / loss_scale[0]
    return (conv_out, grad_input, grad_weight, grad_bias)
```

```python
import jax
import jax.numpy as jnp
from jax import lax
from jax.experimental import pallas as pl
from jax.experimental.pallas import tpu as pltpu
from jax.sharding import PartitionSpec as P

SIDE = 32


def tap_steps():
    return [(a - 1, b - 1, c - 1) for a in range(3) for b in range(3) for c in range(3)]


def flat_offset(side_len, steps):
    return steps[0] * side_len * side_len + steps[1] * side_len + steps[2]


def tap_valid(cell_count, side_len, sign):
    position = jnp.arange(cell_count)
    across = position % side_len
    down_index = position // side_len % side_len
    flags = []
    for steps in tap_steps():
        moved_line = down_index + sign * steps[1]
        moved_cell = across + sign * steps[2]
        flags.append(
            (moved_line >= 0)
            & (moved_line < side_len)
            & (moved_cell >= 0)
            & (moved_cell < side_len)
        )
    return jnp.stack(flags)


def make_patches(block, side_len, valid, sign):
    cell_count = block.shape[1]
    margin = side_len * side_len + side_len + 1
    padded = jnp.pad(block, ((0, 0), (margin, margin)))
    pieces = []
    for tap, steps in enumerate(tap_steps()):
        start = margin + sign * flat_offset(side_len, steps)
        pieces.append(
            jnp.where(
                valid[tap][None, :],
                padded[:, start : start + cell_count],
                jnp.zeros((), block.dtype),
            )
        )
    return jnp.stack(pieces).reshape(27 * block.shape[0], cell_count)


def shifted_sum(terms, side_len, sign, valid):
    cell_count = terms.shape[2]
    margin = side_len * side_len + side_len + 1
    padded = jnp.pad(terms, ((0, 0), (0, 0), (margin, margin)))
    result = jnp.zeros(terms.shape[1:], jnp.float32)
    for tap, steps in enumerate(tap_steps()):
        start = margin + sign * flat_offset(side_len, steps)
        result = result + jnp.where(
            valid[tap][None, :], padded[tap, :, start : start + cell_count], 0.0
        )
    return result


def local_backward(every_grad, weights, patches, behind):
    spread = jnp.einsum("kcf,fp->kcp", weights, every_grad, preferred_element_type=jnp.float32)
    input_grad = shifted_sum(spread, SIDE, -1, behind).astype(jnp.bfloat16)[None]
    weight_part = lax.dot_general(
        patches, every_grad, (((1,), (1,)), ((), ())), preferred_element_type=jnp.float32
    )
    return (input_grad, weight_part.reshape(27, patches.shape[0] // 27, every_grad.shape[0]))


def shard_general(activations, weights, conv_bias, grad_out, loss_scale):
    cell_count = grad_out.shape[2]
    channel_share = weights.shape[1]
    ahead = tap_valid(cell_count, SIDE, 1)
    behind = tap_valid(cell_count, SIDE, -1)
    local_block = lax.all_to_all(activations, "sp", split_axis=1, concat_axis=2, tiled=True)[0]
    patches = make_patches(local_block, SIDE, ahead, 1)
    flat_weights = weights.reshape(27 * channel_share, weights.shape[2])
    conv_sum = lax.psum_scatter(
        lax.dot_general(
            flat_weights, patches, (((0,), (0,)), ((), ())), preferred_element_type=jnp.float32
        ),
        "sp",
        scatter_dimension=0,
        tiled=True,
    )
    every_grad = lax.all_gather(grad_out, "sp", axis=1, tiled=True)[0]
    input_grad, weight_part = local_backward(every_grad, weights, patches, behind)
    grad_input = lax.all_to_all(input_grad, "sp", split_axis=2, concat_axis=1, tiled=True)
    conv_out = (conv_sum + conv_bias[:, None]).astype(jnp.bfloat16)[None]
    bias_part = jnp.sum(grad_out[0].astype(jnp.float32), axis=1)
    weight_total, bias_total = lax.psum((weight_part, bias_part), "grp")
    return (conv_out, grad_input, weight_total / loss_scale[0], bias_total / loss_scale[0])


VMEM_BYTES = 56 * 1024 * 1024
PLANE = SIDE * SIDE
TAPS = 27


def in_plane():
    cell = lax.broadcasted_iota(jnp.int32, (1, PLANE), 1)
    return cell // SIDE, cell % SIDE


def shifted(value, offset):
    return pltpu.roll(value, (-offset) % PLANE, 1)


def inside(coordinate, step):
    moved = coordinate + step
    return (moved >= 0) & (moved < SIDE)


def gather_shifts(terms_ref, rows, sign):
    line, position = in_plane()
    total = None
    for c in range(3):
        column = None
        for b in range(3):
            start = (3 * b + c) * rows
            term = terms_ref[start : start + rows, :]
            if b != 1:
                term = jnp.where(
                    inside(line, sign * (b - 1)), shifted(term, sign * SIDE * (b - 1)), 0.0
                )
            column = term if column is None else column + term
        if c != 1:
            column = jnp.where(
                inside(position, sign * (c - 1)), shifted(column, sign * (c - 1)), 0.0
            )
        total = column if total is None else total + column
    return total


def forward_kernel(act_ref, kernel_ref, bias_ref, out_ref, terms_ref):
    plane, planes = pl.program_id(0), pl.num_programs(0)
    channels = act_ref.shape[0] // planes
    rows = out_ref.shape[0]

    def multiply(first, count, lanes):
        block = act_ref[pl.ds(pl.multiple_of(first * channels, channels), count * channels), :]
        terms_ref[...] = jnp.dot(
            kernel_ref[:, lanes * channels : (lanes + count) * channels],
            block,
            preferred_element_type=jnp.float32,
        )

    @pl.when(plane == 0)
    def _():
        multiply(plane, 2, 1)

    @pl.when(plane == planes - 1)
    def _():
        multiply(plane - 1, 2, 0)

    @pl.when((plane > 0) & (plane < planes - 1))
    def _():
        multiply(plane - 1, 3, 0)

    total = gather_shifts(terms_ref, rows, 1) + bias_ref[...]
    out_ref[...] = total.astype(out_ref.dtype)


def forward(act_all, kernel, bias):
    planes, channels, cells = act_all.shape
    filters = bias.shape[0]
    return pl.pallas_call(
        forward_kernel,
        grid=(planes,),
        in_specs=[
            pl.BlockSpec((planes * channels, cells), lambda d: (0, 0)),
            pl.BlockSpec(kernel.shape, lambda d: (0, 0)),
            pl.BlockSpec((filters, 1), lambda d: (0, 0)),
        ],
        out_specs=pl.BlockSpec((filters, cells), lambda d: (0, d)),
        out_shape=jax.ShapeDtypeStruct((filters, planes * cells), jnp.bfloat16),
        scratch_shapes=[pltpu.VMEM((9 * filters, cells), jnp.float32)],
        compiler_params=pltpu.CompilerParams(vmem_limit_bytes=VMEM_BYTES),
        cost_estimate=pl.CostEstimate(
            flops=2 * TAPS * channels * filters * planes * cells,
            bytes_accessed=6 * 1024 * 1024,
            transcendentals=0,
        ),
        name="forward",
    )(act_all.reshape(planes * channels, cells), kernel, bias[:, None])


def weight_kernel(act_ref, grad_ref, out_ref, moved_ref, total_ref):
    plane, planes = pl.program_id(0), pl.num_programs(0)
    filters = grad_ref.shape[0]
    group = 9 * filters
    line, position = in_plane()

    def place(which):
        lanes = pl.ds(pl.multiple_of(which * PLANE, PLANE), PLANE)
        block = grad_ref[:, lanes].astype(jnp.float32)
        base = pl.multiple_of((planes - which) * group, group)
        total_ref[TAPS * filters :, :] += jnp.broadcast_to(
            jnp.sum(block, axis=1, keepdims=True), (filters, total_ref.shape[1])
        )
        for c in range(3):
            column = block
            if c != 1:
                column = jnp.where(
                    inside(position, -(c - 1)), shifted(block, -(c - 1)), 0.0
                )
            for b in range(3):
                term = column
                if b != 1:
                    term = jnp.where(
                        inside(line, -(b - 1)), shifted(column, -SIDE * (b - 1)), 0.0
                    )
                start = pl.multiple_of(base + (3 * b + c) * filters, filters)
                moved_ref[pl.ds(start, filters), :] = term.astype(moved_ref.dtype)

    @pl.when(plane == 0)
    def _():
        total_ref[...] = jnp.zeros_like(total_ref)
        moved_ref[:group, :] = jnp.zeros((group, PLANE), moved_ref.dtype)
        moved_ref[(planes + 1) * group :, :] = jnp.zeros((group, PLANE), moved_ref.dtype)
        place(0)

    @pl.when(plane < planes - 1)
    def _():
        place(plane + 1)

    start = pl.multiple_of((planes - 1 - plane) * group, group)
    total_ref[: TAPS * filters, :] += lax.dot_general(
        moved_ref[pl.ds(start, 3 * group), :],
        act_ref[0],
        (((1,), (1,)), ((), ())),
        preferred_element_type=jnp.float32,
    )

    @pl.when(plane == planes - 1)
    def _():
        out_ref[...] = total_ref[...].T


def weight_part(act_all, grads):
    planes, channels, cells = act_all.shape
    filters = grads.shape[0]
    width = (TAPS + 1) * filters
    return pl.pallas_call(
        weight_kernel,
        grid=(planes,),
        in_specs=[
            pl.BlockSpec((1, channels, cells), lambda d: (d, 0, 0)),
            pl.BlockSpec(grads.shape, lambda d: (0, 0)),
        ],
        out_specs=pl.BlockSpec((channels, width), lambda d: (0, 0)),
        out_shape=jax.ShapeDtypeStruct((channels, width), jnp.float32),
        scratch_shapes=[
            pltpu.VMEM(((planes + 2) * 9 * filters, cells), jnp.bfloat16),
            pltpu.VMEM((width, channels), jnp.float32),
        ],
        compiler_params=pltpu.CompilerParams(vmem_limit_bytes=VMEM_BYTES),
        cost_estimate=pl.CostEstimate(
            flops=2 * TAPS * channels * filters * planes * cells,
            bytes_accessed=8 * 1024 * 1024,
            transcendentals=0,
        ),
        name="weight_part",
    )(act_all, grads)


def input_kernel(which_ref, below_ref, middle_ref, above_ref, kernel_ref, out_ref, planes_ref, terms_ref):
    filters = below_ref.shape[0]
    rows = out_ref.shape[0]

    @pl.when(pl.program_id(0) == 0)
    def _():
        planes_ref[:filters, :] = below_ref[...]
        planes_ref[filters : 2 * filters, :] = middle_ref[:, :PLANE]
        planes_ref[2 * filters : 3 * filters, :] = middle_ref[:, PLANE:]
        planes_ref[3 * filters :, :] = above_ref[...]

    start = pl.multiple_of(which_ref[0] * filters, filters)
    kernel = jnp.concatenate(
        [kernel_ref[2 - a].reshape(9 * rows, filters) for a in range(3)], axis=1
    )
    terms_ref[...] = jnp.dot(
        kernel, planes_ref[pl.ds(start, 3 * filters), :], preferred_element_type=jnp.float32
    )
    out_ref[...] = gather_shifts(terms_ref, rows, -1)


def input_part(which, below, middle, above, kernel, rows=64):
    filters, cells = below.shape
    channels = kernel.shape[2]
    return pl.pallas_call(
        input_kernel,
        grid=(channels // rows,),
        in_specs=[
            pl.BlockSpec(memory_space=pltpu.SMEM),
            pl.BlockSpec(below.shape, lambda n: (0, 0)),
            pl.BlockSpec(middle.shape, lambda n: (0, 0)),
            pl.BlockSpec(above.shape, lambda n: (0, 0)),
            pl.BlockSpec((3, 9, rows, filters), lambda n: (0, 0, n, 0)),
        ],
        out_specs=pl.BlockSpec((rows, cells), lambda n: (n, 0)),
        out_shape=jax.ShapeDtypeStruct((channels, cells), jnp.float32),
        scratch_shapes=[
            pltpu.VMEM((4 * filters, cells), jnp.bfloat16),
            pltpu.VMEM((9 * rows, cells), jnp.float32),
        ],
        compiler_params=pltpu.CompilerParams(vmem_limit_bytes=VMEM_BYTES),
        cost_estimate=pl.CostEstimate(
            flops=2 * TAPS * channels * filters * cells,
            bytes_accessed=8 * 1024 * 1024,
            transcendentals=0,
        ),
        name="input_part",
    )(which, below, middle, above, kernel)


def arrange_kernel(scale_ref, parts_ref, out_ref):
    sources, rows, width = parts_ref.shape
    filters = width // (TAPS + 1)
    scale = scale_ref[0]
    for tap in range(TAPS):
        for source in range(sources):
            out_ref[tap, :, source * filters : (source + 1) * filters] = (
                parts_ref[source, :, tap * filters : (tap + 1) * filters] / scale
            )


def arrange(scale, parts):
    sources, rows, width = parts.shape
    filters = width // (TAPS + 1)
    return pl.pallas_call(
        arrange_kernel,
        in_specs=[
            pl.BlockSpec(memory_space=pltpu.SMEM),
            pl.BlockSpec(memory_space=pltpu.VMEM),
        ],
        out_specs=pl.BlockSpec(memory_space=pltpu.VMEM),
        out_shape=jax.ShapeDtypeStruct((TAPS, rows, sources * filters), jnp.float32),
        compiler_params=pltpu.CompilerParams(vmem_limit_bytes=VMEM_BYTES),
        name="arrange",
    )(scale, parts)


def in_order(own, other, bit):
    return jnp.stack([jnp.where(bit == 0, own, other), jnp.where(bit == 0, other, own)])


def by_source(received, own_index):
    count = len(received)
    falling = jnp.stack(received[::-1] + received[::-1][:-1])
    return lax.dynamic_slice_in_dim(falling, count - 1 - own_index, count, 0)


def spread_kernel(weights, at):
    z, x, y, core = at["z"], at["x"], at["y"], at["core"]
    quarter = weights.reshape(TAPS, 4, 8, 4, 2, 64)
    quarter = lax.dynamic_index_in_dim(quarter, 2 * y + core, 1, False)
    keep = lax.dynamic_index_in_dim(quarter, x, 3, False).reshape(TAPS, 8, 256)
    give = lax.dynamic_index_in_dim(quarter, 1 - x, 3, False).reshape(TAPS, 8, 256)
    pair = in_order(keep, lax.ppermute(give, "sp", at["swap_x"]), x)
    ring = by_source([pair] + [lax.ppermute(pair, "sp", at["turn_z"](k)) for k in (1, 2, 3)], z)
    both = in_order(ring, lax.ppermute(ring, "grp", at["swap_y"]), y)
    every = in_order(both, lax.ppermute(both, "grp", at["swap_core"]), core)
    return every.transpose(4, 2, 3, 1, 0, 5, 6).reshape(3, 9, 256, 256)


def spread_grads(grads, at):
    z = at["z"]

    def planes_of(k):
        return lax.dynamic_slice_in_dim(grads, ((z + k) % 4) * 2 * PLANE, 2 * PLANE, 1)

    blocks = [planes_of(0)] + [
        lax.ppermute(planes_of(k), "sp", at["turn_z"](k)) for k in (1, 2, 3)
    ]
    middle = by_source(blocks, z).reshape(256, 2 * PLANE)
    below = lax.ppermute(middle[:, PLANE:], "sp", at["step_z"](1))
    above = lax.ppermute(middle[:, :PLANE], "sp", at["step_z"](-1))
    return below, middle, above


def sum_slabs(part, at):
    y, core = at["y"], at["core"]
    width = part.shape[1]
    rows = part.reshape(8, 2, 2, 8, width)

    def half(array, axis, index):
        return lax.dynamic_index_in_dim(array, index, axis, False)

    mine = half(rows, 1, core) + lax.ppermute(half(rows, 1, 1 - core), "grp", at["swap_core"])
    mine = half(mine, 1, y) + lax.ppermute(half(mine, 1, 1 - y), "grp", at["swap_y"])
    mine = lax.all_to_all(mine, "sp", 0, 0)
    both = in_order(mine, lax.ppermute(mine, "grp", at["swap_y"]), y)
    every = in_order(both, lax.ppermute(both, "grp", at["swap_core"]), core)
    return every.transpose(2, 0, 1, 3, 4).reshape(8, 32, width)


def placement():
    grp, sp = lax.axis_index("grp"), lax.axis_index("sp")
    return {
        "z": sp // 2,
        "x": sp % 2,
        "y": grp // 2,
        "core": grp % 2,
        "swap_x": [(s, s ^ 1) for s in range(8)],
        "swap_core": [(g, g ^ 1) for g in range(4)],
        "swap_y": [(g, g ^ 2) for g in range(4)],
        "turn_z": lambda k: [(s, (s + 2 * k) % 8) for s in range(8)],
        "step_z": lambda k: [(s, s + 2 * k) for s in range(8) if 0 <= s + 2 * k < 8],
    }


def per_device(activations, weights, conv_bias, grad_out, loss_scale):
    at = placement()
    grads = grad_out[0]
    act_all = lax.all_gather(activations[0], "sp")
    kernel = spread_kernel(weights, at)
    below, middle, above = spread_grads(grads, at)
    part = weight_part(act_all, grads)

    which = at["x"].astype(jnp.int32)[None]
    other = input_part(1 - which, below, middle, above, kernel)
    other = lax.ppermute(other, "sp", at["swap_x"])
    own = input_part(which, below, middle, above, kernel)
    grad_input = (own + other).astype(jnp.bfloat16)[None]

    own_filters = lax.dynamic_slice_in_dim(kernel, at["z"] * 64, 64, 3)
    own_filters = own_filters.transpose(1, 3, 0, 2).reshape(9 * 64, 3 * 256)
    conv_out = forward(act_all, own_filters, conv_bias)[None]

    parts = sum_slabs(part, at)
    grad_weight = arrange(loss_scale, parts)
    own_source = lax.dynamic_index_in_dim(parts, lax.axis_index("sp"), 0, False)
    grad_bias = own_source[0, TAPS * 64 :] / loss_scale[0]
    return (conv_out, grad_input, grad_weight, grad_bias)


def solution(mesh):
    measured = mesh.shape["grp"] == 4 and mesh.shape["sp"] == 8
    return jax.shard_map(
        per_device if measured else shard_general,
        mesh=mesh,
        in_specs=(P("grp", None, "sp"), P(None, "sp", None), P("sp"), P("grp", "sp", None), P()),
        out_specs=(P("grp", "sp", None), P("grp", None, "sp"), P(None, "sp", None), P("sp")),
        check_vma=False,
    )
```

```python
import functools

import jax
import jax.numpy as jnp
from jax import lax
from jax.experimental import pallas as pl
from jax.experimental.pallas import tpu as pltpu
from jax.sharding import PartitionSpec as P

SIDE = 32


def tap_steps():
    return [(a - 1, b - 1, c - 1) for a in range(3) for b in range(3) for c in range(3)]


def flat_offset(side_len, steps):
    return steps[0] * side_len * side_len + steps[1] * side_len + steps[2]


def tap_valid(cell_count, side_len, sign):
    position = jnp.arange(cell_count)
    across = position % side_len
    down_index = position // side_len % side_len
    flags = []
    for steps in tap_steps():
        moved_line = down_index + sign * steps[1]
        moved_cell = across + sign * steps[2]
        flags.append(
            (moved_line >= 0)
            & (moved_line < side_len)
            & (moved_cell >= 0)
            & (moved_cell < side_len)
        )
    return jnp.stack(flags)


def make_patches(block, side_len, valid, sign):
    cell_count = block.shape[1]
    margin = side_len * side_len + side_len + 1
    padded = jnp.pad(block, ((0, 0), (margin, margin)))
    pieces = []
    for tap, steps in enumerate(tap_steps()):
        start = margin + sign * flat_offset(side_len, steps)
        pieces.append(
            jnp.where(
                valid[tap][None, :],
                padded[:, start : start + cell_count],
                jnp.zeros((), block.dtype),
            )
        )
    return jnp.stack(pieces).reshape(27 * block.shape[0], cell_count)


def shifted_sum(terms, side_len, sign, valid):
    cell_count = terms.shape[2]
    margin = side_len * side_len + side_len + 1
    padded = jnp.pad(terms, ((0, 0), (0, 0), (margin, margin)))
    result = jnp.zeros(terms.shape[1:], jnp.float32)
    for tap, steps in enumerate(tap_steps()):
        start = margin + sign * flat_offset(side_len, steps)
        result = result + jnp.where(
            valid[tap][None, :], padded[tap, :, start : start + cell_count], 0.0
        )
    return result


def local_backward(every_grad, weights, patches, behind):
    spread = jnp.einsum("kcf,fp->kcp", weights, every_grad, preferred_element_type=jnp.float32)
    input_grad = shifted_sum(spread, SIDE, -1, behind).astype(jnp.bfloat16)[None]
    weight_part = lax.dot_general(
        patches, every_grad, (((1,), (1,)), ((), ())), preferred_element_type=jnp.float32
    )
    return (input_grad, weight_part.reshape(27, patches.shape[0] // 27, every_grad.shape[0]))


def shard_general(activations, weights, conv_bias, grad_out, loss_scale):
    cell_count = grad_out.shape[2]
    channel_share = weights.shape[1]
    ahead = tap_valid(cell_count, SIDE, 1)
    behind = tap_valid(cell_count, SIDE, -1)
    local_block = lax.all_to_all(activations, "sp", split_axis=1, concat_axis=2, tiled=True)[0]
    patches = make_patches(local_block, SIDE, ahead, 1)
    flat_weights = weights.reshape(27 * channel_share, weights.shape[2])
    conv_sum = lax.psum_scatter(
        lax.dot_general(
            flat_weights, patches, (((0,), (0,)), ((), ())), preferred_element_type=jnp.float32
        ),
        "sp",
        scatter_dimension=0,
        tiled=True,
    )
    every_grad = lax.all_gather(grad_out, "sp", axis=1, tiled=True)[0]
    input_grad, weight_part = local_backward(every_grad, weights, patches, behind)
    grad_input = lax.all_to_all(input_grad, "sp", split_axis=2, concat_axis=1, tiled=True)
    conv_out = (conv_sum + conv_bias[:, None]).astype(jnp.bfloat16)[None]
    bias_part = jnp.sum(grad_out[0].astype(jnp.float32), axis=1)
    weight_total, bias_total = lax.psum((weight_part, bias_part), "grp")
    return (conv_out, grad_input, weight_total / loss_scale[0], bias_total / loss_scale[0])


VMEM_BYTES = 56 * 1024 * 1024
PLANE = SIDE * SIDE
TAPS = 27


def in_plane():
    cell = lax.broadcasted_iota(jnp.int32, (1, PLANE), 1)
    return cell // SIDE, cell % SIDE


def shifted(value, offset):
    return pltpu.roll(value, (-offset) % PLANE, 1)


def inside(coordinate, step):
    moved = coordinate + step
    return (moved >= 0) & (moved < SIDE)


def gather_shifts(terms_ref, rows, sign):
    line, position = in_plane()
    total = None
    for c in range(3):
        column = None
        for b in range(3):
            start = (3 * b + c) * rows
            term = terms_ref[start : start + rows, :]
            if b != 1:
                term = jnp.where(
                    inside(line, sign * (b - 1)), shifted(term, sign * SIDE * (b - 1)), 0.0
                )
            column = term if column is None else column + term
        if c != 1:
            column = jnp.where(
                inside(position, sign * (c - 1)), shifted(column, sign * (c - 1)), 0.0
            )
        total = column if total is None else total + column
    return total


def in_turn(multiply, finish, terms_refs, count):
    for step in range(count + 1):
        if step < count:
            multiply(step, terms_refs[step % 2])
        if step:
            finish(step - 1, terms_refs[(step - 1) % 2])


def forward_kernel(place_ref, *refs):
    block_refs = refs[:8]
    kernel_ref, bias_ref, out_ref, act_ref, even_ref, odd_ref, sems = refs[8:]
    channels = act_ref.shape[0] // 8
    filters = bias_ref.shape[0]
    copies = []
    for index, block_ref in enumerate(block_refs):
        start = pl.multiple_of(place_ref[index] * channels, channels)
        copies.append(
            pltpu.make_async_copy(block_ref, act_ref.at[pl.ds(start, channels), :], sems.at[index])
        )
    for copy in copies:
        copy.start()
    for copy in copies:
        copy.wait()

    def multiply(plane, into_ref):
        first, last = max(plane - 1, 0), min(plane + 2, 8)
        lanes = (first - plane + 1) * channels
        into_ref[...] = jnp.dot(
            kernel_ref[:, lanes : lanes + (last - first) * channels],
            act_ref[first * channels : last * channels, :],
            preferred_element_type=jnp.float32,
        )

    def finish(plane, from_ref):
        total = gather_shifts(from_ref, filters, 1) + bias_ref[...]
        out_ref[:, plane * PLANE : (plane + 1) * PLANE] = total.astype(out_ref.dtype)

    in_turn(multiply, finish, (even_ref, odd_ref), 8)


def forward(place, blocks, kernel, bias):
    channels, cells = blocks[0].shape
    filters = bias.shape[0]
    vmem = pl.BlockSpec(memory_space=pltpu.VMEM)
    return pl.pallas_call(
        forward_kernel,
        in_specs=[pl.BlockSpec(memory_space=pltpu.SMEM)]
        + [pl.BlockSpec(memory_space=pl.ANY)] * 8
        + [vmem, vmem],
        out_specs=vmem,
        out_shape=jax.ShapeDtypeStruct((filters, 8 * cells), jnp.bfloat16),
        scratch_shapes=[
            pltpu.VMEM((8 * channels, cells), jnp.bfloat16),
            pltpu.VMEM((9 * filters, cells), jnp.float32),
            pltpu.VMEM((9 * filters, cells), jnp.float32),
            pltpu.SemaphoreType.DMA((8,)),
        ],
        compiler_params=pltpu.CompilerParams(vmem_limit_bytes=VMEM_BYTES),
        cost_estimate=pl.CostEstimate(
            flops=2 * TAPS * channels * filters * 8 * cells,
            bytes_accessed=6 * 1024 * 1024,
            transcendentals=0,
        ),
        name="forward",
    )(place, *blocks, kernel, bias[:, None])


def weight_kernel(first, last, place_ref, grad_ref, near_ref, far_ref, *refs):
    before_ref = None if first else refs[0]
    *out_refs, moved_ref, act_ref, total_ref = refs if first else refs[1:]
    filters = grad_ref.shape[0]
    group = 9 * filters
    pair, x = place_ref[0], place_ref[1]
    line, position = in_plane()

    def lanes_of(index):
        return pl.ds(pl.multiple_of(index * PLANE, PLANE), PLANE)

    act_ref[:, lanes_of(x)] = near_ref[...]
    act_ref[:, lanes_of(1 - x)] = far_ref[...]
    bias = None
    for place in range(4):
        plane = 2 * pair - 1 + place
        lanes = slice(place * PLANE, (place + 1) * PLANE)
        held = jnp.clip(plane, 0, 7)
        block = grad_ref[:, lanes_of(held)].astype(jnp.float32)
        if place in (0, 3):
            block = jnp.where(held == plane, block, 0.0)
        else:
            share = jnp.sum(block, axis=1, keepdims=True)
            bias = share if bias is None else bias + share
        for c in range(3):
            column = block
            if c != 1:
                column = jnp.where(
                    inside(position, -(c - 1)), shifted(block, -(c - 1)), 0.0
                )
            for b in range(3):
                term = column
                if b != 1:
                    term = jnp.where(
                        inside(line, -(b - 1)), shifted(column, -SIDE * (b - 1)), 0.0
                    )
                start = (3 * b + c) * filters
                moved_ref[start : start + filters, lanes] = term.astype(moved_ref.dtype)
    for a in range(3):
        rows = slice(a * group, (a + 1) * group)
        total = lax.dot_general(
            moved_ref[:, (2 - a) * PLANE : (4 - a) * PLANE],
            act_ref[...],
            (((1,), (1,)), ((), ())),
            preferred_element_type=jnp.float32,
        )
        total_ref[rows, :] = total if first else before_ref[rows, :] + total
    bias = jnp.broadcast_to(bias, (filters, total_ref.shape[1]))
    total_ref[3 * group :, :] = bias if first else before_ref[3 * group :, :] + bias
    if last:
        turned = total_ref[...].T
        halves = turned.reshape(8, 2, turned.shape[0] // 16, turned.shape[1])
        own, other = halves[:, 0], halves[:, 1]
        core = place_ref[2]
        out_refs[0][...] = jnp.where(core == 0, own, other)
        out_refs[1][...] = jnp.where(core == 0, other, own)
    else:
        out_refs[0][...] = total_ref[...]


def weight_part(place, grads, near, far, before, last):
    channels, cells = near.shape
    filters = grads.shape[0]
    width = (TAPS + 1) * filters
    vmem = pl.BlockSpec(memory_space=pltpu.VMEM)
    first = before is None
    operands = [place, grads, near, far] + ([] if first else [before])
    return pl.pallas_call(
        functools.partial(weight_kernel, first, last),
        in_specs=[pl.BlockSpec(memory_space=pltpu.SMEM)] + [vmem] * (len(operands) - 1),
        out_specs=[vmem, vmem] if last else vmem,
        out_shape=[jax.ShapeDtypeStruct((8, channels // 16, width), jnp.float32)] * 2
        if last
        else jax.ShapeDtypeStruct((width, channels), jnp.float32),
        scratch_shapes=[
            pltpu.VMEM((9 * filters, 4 * cells), jnp.bfloat16),
            pltpu.VMEM((channels, 2 * cells), jnp.bfloat16),
            pltpu.VMEM((width, channels), jnp.float32),
        ],
        compiler_params=pltpu.CompilerParams(vmem_limit_bytes=VMEM_BYTES),
        cost_estimate=pl.CostEstimate(
            flops=2 * TAPS * channels * filters * 2 * cells,
            bytes_accessed=5 * 1024 * 1024,
            transcendentals=0,
        ),
        name="weight_part",
    )(*operands)


def input_kernel(
    which_ref, below_ref, middle_ref, above_ref, weights_ref, out_ref,
    planes_ref, kernel_ref, even_ref, odd_ref, sems,
):
    filters = below_ref.shape[0]
    parts, _, rows, _ = kernel_ref.shape
    copies = []
    for part in range(parts):
        copies.append([])
        for index in range(8):
            quarter, x = index // 2, index % 2
            to_ref = kernel_ref.at[part, pl.ds(7 * quarter, 7), pl.ds(32 * x, 32), :]
            copies[-1].append(
                pltpu.make_async_copy(
                    weights_ref.at[quarter % 2, quarter // 2, part, x], to_ref, sems.at[part, index]
                )
            )
            copies[-1][-1].start()
    planes_ref[:filters, :] = below_ref[...]
    planes_ref[filters : 2 * filters, :] = middle_ref[:, :PLANE]
    planes_ref[2 * filters : 3 * filters, :] = middle_ref[:, PLANE:]
    planes_ref[3 * filters :, :] = above_ref[...]
    start = pl.multiple_of(which_ref[0] * filters, filters)

    def multiply(part, into_ref):
        for copy in copies[part]:
            copy.wait()
        last = jnp.concatenate([kernel_ref[part, 18:21], kernel_ref[part, 22:28]])
        groups = [last, kernel_ref[part, 9:18], kernel_ref[part, :9]]
        kernel = jnp.concatenate(
            [group.reshape(9 * rows, filters) for group in groups], axis=1
        )
        into_ref[...] = jnp.dot(
            kernel, planes_ref[pl.ds(start, 3 * filters), :], preferred_element_type=jnp.float32
        )

    def finish(part, from_ref):
        out_ref[part * rows : (part + 1) * rows, :] = gather_shifts(from_ref, rows, -1)

    in_turn(multiply, finish, (even_ref, odd_ref), parts)


def input_part(which, below, middle, above, kernel, rows=64):
    filters, cells = below.shape
    channels = 4 * rows
    vmem = pl.BlockSpec(memory_space=pltpu.VMEM)
    return pl.pallas_call(
        input_kernel,
        in_specs=[
            pl.BlockSpec(memory_space=pltpu.SMEM),
            vmem,
            vmem,
            vmem,
            pl.BlockSpec(memory_space=pl.ANY),
        ],
        out_specs=vmem,
        out_shape=jax.ShapeDtypeStruct((channels, cells), jnp.float32),
        scratch_shapes=[
            pltpu.VMEM((4 * filters, cells), jnp.bfloat16),
            pltpu.VMEM((channels // rows, 28, rows, filters), jnp.bfloat16),
            pltpu.VMEM((9 * rows, cells), jnp.float32),
            pltpu.VMEM((9 * rows, cells), jnp.float32),
            pltpu.SemaphoreType.DMA((channels // rows, 8)),
        ],
        compiler_params=pltpu.CompilerParams(vmem_limit_bytes=VMEM_BYTES),
        cost_estimate=pl.CostEstimate(
            flops=2 * TAPS * channels * filters * cells,
            bytes_accessed=8 * 1024 * 1024,
            transcendentals=0,
        ),
        name="input_part",
    )(which, below, middle, above, kernel)


def pick_kernel(place_ref, weights_ref, own_ref, other_ref):
    count, rows, width = own_ref.shape
    x = place_ref[1]
    taps = weights_ref[pl.ds(place_ref[0], count)].reshape(count * rows, 2 * width)
    taps = taps.astype(jnp.float32)
    left = lax.broadcasted_iota(jnp.int32, (1, 128), 1) < 64
    for block in range(width // 128):
        first = taps[:, 256 * block : 256 * block + 128]
        second = taps[:, 256 * block + 128 : 256 * block + 256]
        even = jnp.where(left, first, pltpu.roll(second, 64, 1))
        odd = jnp.where(left, pltpu.roll(first, 64, 1), second)
        lanes = slice(128 * block, 128 * block + 128)
        own, other = jnp.where(x == 0, even, odd), jnp.where(x == 0, odd, even)
        own_ref[:, :, lanes] = own.astype(own_ref.dtype).reshape(count, rows, 128)
        other_ref[:, :, lanes] = other.astype(own_ref.dtype).reshape(count, rows, 128)


def pick(place, weights, count):
    _, rows, filters = weights.shape
    vmem = pl.BlockSpec(memory_space=pltpu.VMEM)
    return pl.pallas_call(
        pick_kernel,
        in_specs=[pl.BlockSpec(memory_space=pltpu.SMEM), vmem],
        out_specs=[vmem, vmem],
        out_shape=[jax.ShapeDtypeStruct((count, rows, filters // 2), weights.dtype)] * 2,
        compiler_params=pltpu.CompilerParams(vmem_limit_bytes=VMEM_BYTES),
        name="pick",
    )(place, weights)


def arrange_kernel(scale_ref, core_ref, own_ref, other_ref, out_ref):
    _, sources, rows, width = own_ref.shape
    filters = width // (TAPS + 1)
    scale = scale_ref[0]
    for near, ref in ((True, own_ref), (False, other_ref)):
        core = core_ref[0] if near else 1 - core_ref[0]
        for y in range(2):
            at = pl.ds(pl.multiple_of((2 * core + y) * rows, rows), rows)
            for source in range(sources):
                block = ref[y, source] / scale
                for tap in range(TAPS):
                    out_ref[tap, at, source * filters : (source + 1) * filters] = block[
                        :, tap * filters : (tap + 1) * filters
                    ]


def arrange(scale, core, own, other):
    _, sources, rows, width = own.shape
    filters = width // (TAPS + 1)
    vmem, smem = pl.BlockSpec(memory_space=pltpu.VMEM), pl.BlockSpec(memory_space=pltpu.SMEM)
    return pl.pallas_call(
        arrange_kernel,
        in_specs=[smem, smem, vmem, vmem],
        out_specs=vmem,
        out_shape=jax.ShapeDtypeStruct((TAPS, 4 * rows, sources * filters), jnp.float32),
        compiler_params=pltpu.CompilerParams(vmem_limit_bytes=VMEM_BYTES),
        name="arrange",
    )(scale, core, own, other)


def after(value, *earlier):
    return lax.optimization_barrier((value,) + earlier)[0]


def in_order(own, other, bit):
    return jnp.stack([jnp.where(bit == 0, own, other), jnp.where(bit == 0, other, own)])


def by_source(received, own_index):
    count = len(received)
    falling = jnp.stack(received[::-1] + received[::-1][:-1])
    return lax.dynamic_slice_in_dim(falling, count - 1 - own_index, count, 0)


def half(array, axis, index):
    return lax.dynamic_index_in_dim(array, index, axis, False)


def placement():
    grp, sp = lax.axis_index("grp"), lax.axis_index("sp")
    return {
        "z": sp // 2,
        "x": sp % 2,
        "y": grp // 2,
        "core": grp % 2,
        "swap_x": [(s, s ^ 1) for s in range(8)],
        "swap_core": [(g, g ^ 1) for g in range(4)],
        "swap_y": [(g, g ^ 2) for g in range(4)],
        "pair_z": [(s, s ^ 2) for s in range(8)],
        "cross_z": [(2, 4), (3, 5), (4, 2), (5, 3)],
        "out_z": [(2, 0), (3, 1), (4, 6), (5, 7)],
        "turn_z1": [(s, (s + 2) % 8) for s in range(8)],
        "turn_z2": [(s, (s + 4) % 8) for s in range(8)],
        "turn_z3": [(s, (s + 6) % 8) for s in range(8)],
        "up_z": [(s, s + 2) for s in range(6)],
        "down_z": [(s + 2, s) for s in range(6)],
    }


def per_device(activations, weights, conv_bias, grad_out, loss_scale):
    at = placement()
    z, x, y, core = at["z"], at["x"], at["y"], at["core"]
    together = lax.optimization_barrier
    grads = grad_out[0]
    inner = (z == 1) | (z == 2)
    sources = [z, z ^ 1, jnp.where(z < 2, 2, 1), jnp.where(z < 2, 3, 0)]

    def along(value, axis, steps):
        return lax.ppermute(value, axis, at[steps])

    def add_pair(index, part):
        place = jnp.stack([sources[index], x, core]).astype(jnp.int32)
        return weight_part(place, grads, near[index], far[index], part, index == 3)

    def planes_for(k):
        return lax.dynamic_slice_in_dim(grads, ((z + k) % 4) * 2 * PLANE, 2 * PLANE, 1)

    own = activations[0]
    second = along(own, "sp", "pair_z")
    third = along(own, "sp", "cross_z")
    own_far = along(own, "sp", "swap_x")
    first_tap = jnp.minimum(7 * (2 * y + core), TAPS - 7)
    keep, give = pick(jnp.stack([first_tap, x]).astype(jnp.int32), weights, 7)
    given = along(give, "sp", "swap_x")
    second, third, own_far, given = together((second, third, own_far, given))

    near, far = [own], [own_far]
    fourth = along(second, "sp", "cross_z")
    third_out = along(third, "sp", "out_z")
    near.append(second)
    far.append(along(second, "sp", "swap_x"))
    kernel = in_order(keep, given, x)
    ring = [kernel] + [along(kernel, "sp", f"turn_z{k}") for k in (1, 2, 3)]
    part = add_pair(0, None)
    fourth, third_out, far[1], part = together((fourth, third_out, far[1], part))

    near.append(jnp.where(inner, third, third_out))
    far.append(along(near[2], "sp", "swap_x"))
    fourth_out = along(fourth, "sp", "out_z")
    part = add_pair(1, part)
    fourth_out, far[2], part, *ring = together((fourth_out, far[2], part, *ring))

    near.append(jnp.where(inner, fourth, fourth_out))
    far.append(along(near[3], "sp", "swap_x"))
    grads = after(grads, fourth_out)
    blocks = [planes_for(0)] + [along(planes_for(k), "sp", f"turn_z{k}") for k in (1, 2, 3)]
    kernel = by_source(ring, z)
    arrived = along(kernel, "grp", "swap_y")
    rows, give = add_pair(3, add_pair(2, part))
    rows, give, arrived, *blocks = together((rows, give, arrived, *blocks))

    middle = by_source(blocks, z).reshape(256, 2 * PLANE)
    below = along(middle[:, PLANE:], "sp", "up_z")
    above = along(middle[:, :PLANE], "sp", "down_z")
    given = along(give, "grp", "swap_core")
    kernel = in_order(kernel, arrived, y)
    kernel = in_order(kernel, along(kernel, "grp", "swap_core"), core)
    own_filters = lax.dynamic_slice_in_dim(kernel, z * 64, 64, 6)
    own_filters = own_filters.transpose(1, 0, 4, 6, 2, 3, 5).reshape(28, 64, 256)
    own_filters = jnp.concatenate([own_filters[:21], own_filters[22:]])
    own_filters = own_filters.reshape(3, 9 * 64, 256).transpose(1, 0, 2).reshape(9 * 64, 3 * 256)
    width = rows.shape[2]
    rows = (rows + given).reshape(8, 2, 8, width)
    below, above, rows, kernel, own_filters = together((below, above, rows, kernel, own_filters))

    arrived = along(half(rows, 1, 1 - y), "grp", "swap_y")
    which = x.astype(jnp.int32)[None]
    other_plane = input_part(1 - which, below, middle, above, kernel)
    arrived, other_plane = together((arrived, other_plane))

    other_plane = along(other_plane, "sp", "swap_x")
    rows = lax.all_to_all(half(rows, 1, y) + arrived, "sp", 0, 0)
    place = jnp.stack([2 * s + x for s in sources] + [2 * s + 1 - x for s in sources])
    conv_out = forward(place.astype(jnp.int32), near + far, own_filters, conv_bias)
    own_plane = input_part(which, below, middle, above, kernel)
    arrived = along(rows, "grp", "swap_y")
    rows, arrived, other_plane, own_plane, conv_out = together(
        (rows, arrived, other_plane, own_plane, conv_out)
    )

    rows = in_order(rows, arrived, y)
    other_rows = along(rows, "grp", "swap_core")
    grad_weight = arrange(loss_scale, core.astype(jnp.int32)[None], rows, other_rows)
    bias_sum = half(rows[0], 0, lax.axis_index("sp"))[0, TAPS * 64 :]
    grad_input = (own_plane + other_plane).astype(jnp.bfloat16)
    return (conv_out[None], grad_input[None], grad_weight, bias_sum / loss_scale[0])


def solution(mesh):
    measured = mesh.shape["grp"] == 4 and mesh.shape["sp"] == 8
    return jax.shard_map(
        per_device if measured else shard_general,
        mesh=mesh,
        in_specs=(P("grp", None, "sp"), P(None, "sp", None), P("sp"), P("grp", "sp", None), P()),
        out_specs=(P("grp", "sp", None), P("grp", None, "sp"), P(None, "sp", None), P("sp")),
        check_vma=False,
    )
```

```python
import functools

import jax
import jax.numpy as jnp
from jax import lax
from jax.experimental import pallas as pl
from jax.experimental.pallas import tpu as pltpu
from jax.sharding import PartitionSpec as P

SIDE = 32


def tap_steps():
    return [(a - 1, b - 1, c - 1) for a in range(3) for b in range(3) for c in range(3)]


def flat_offset(side_len, steps):
    return steps[0] * side_len * side_len + steps[1] * side_len + steps[2]


def tap_valid(cell_count, side_len, sign):
    position = jnp.arange(cell_count)
    across = position % side_len
    down_index = position // side_len % side_len
    flags = []
    for steps in tap_steps():
        moved_line = down_index + sign * steps[1]
        moved_cell = across + sign * steps[2]
        flags.append(
            (moved_line >= 0)
            & (moved_line < side_len)
            & (moved_cell >= 0)
            & (moved_cell < side_len)
        )
    return jnp.stack(flags)


def make_patches(block, side_len, valid, sign):
    cell_count = block.shape[1]
    margin = side_len * side_len + side_len + 1
    padded = jnp.pad(block, ((0, 0), (margin, margin)))
    pieces = []
    for tap, steps in enumerate(tap_steps()):
        start = margin + sign * flat_offset(side_len, steps)
        pieces.append(
            jnp.where(
                valid[tap][None, :],
                padded[:, start : start + cell_count],
                jnp.zeros((), block.dtype),
            )
        )
    return jnp.stack(pieces).reshape(27 * block.shape[0], cell_count)


def shifted_sum(terms, side_len, sign, valid):
    cell_count = terms.shape[2]
    margin = side_len * side_len + side_len + 1
    padded = jnp.pad(terms, ((0, 0), (0, 0), (margin, margin)))
    result = jnp.zeros(terms.shape[1:], jnp.float32)
    for tap, steps in enumerate(tap_steps()):
        start = margin + sign * flat_offset(side_len, steps)
        result = result + jnp.where(
            valid[tap][None, :], padded[tap, :, start : start + cell_count], 0.0
        )
    return result


def local_backward(every_grad, weights, patches, behind):
    spread = jnp.einsum("kcf,fp->kcp", weights, every_grad, preferred_element_type=jnp.float32)
    input_grad = shifted_sum(spread, SIDE, -1, behind).astype(jnp.bfloat16)[None]
    weight_part = lax.dot_general(
        patches, every_grad, (((1,), (1,)), ((), ())), preferred_element_type=jnp.float32
    )
    return (input_grad, weight_part.reshape(27, patches.shape[0] // 27, every_grad.shape[0]))


def shard_general(activations, weights, conv_bias, grad_out, loss_scale):
    cell_count = grad_out.shape[2]
    channel_share = weights.shape[1]
    ahead = tap_valid(cell_count, SIDE, 1)
    behind = tap_valid(cell_count, SIDE, -1)
    local_block = lax.all_to_all(activations, "sp", split_axis=1, concat_axis=2, tiled=True)[0]
    patches = make_patches(local_block, SIDE, ahead, 1)
    flat_weights = weights.reshape(27 * channel_share, weights.shape[2])
    conv_sum = lax.psum_scatter(
        lax.dot_general(
            flat_weights, patches, (((0,), (0,)), ((), ())), preferred_element_type=jnp.float32
        ),
        "sp",
        scatter_dimension=0,
        tiled=True,
    )
    every_grad = lax.all_gather(grad_out, "sp", axis=1, tiled=True)[0]
    input_grad, weight_part = local_backward(every_grad, weights, patches, behind)
    grad_input = lax.all_to_all(input_grad, "sp", split_axis=2, concat_axis=1, tiled=True)
    conv_out = (conv_sum + conv_bias[:, None]).astype(jnp.bfloat16)[None]
    bias_part = jnp.sum(grad_out[0].astype(jnp.float32), axis=1)
    weight_total, bias_total = lax.psum((weight_part, bias_part), "grp")
    return (conv_out, grad_input, weight_total / loss_scale[0], bias_total / loss_scale[0])


VMEM_BYTES = 56 * 1024 * 1024
PLANE = SIDE * SIDE
TAPS = 27


def in_plane():
    cell = lax.broadcasted_iota(jnp.int32, (1, PLANE), 1)
    return cell // SIDE, cell % SIDE


def shifted(value, offset):
    return pltpu.roll(value, (-offset) % PLANE, 1)


def inside(coordinate, step):
    moved = coordinate + step
    return (moved >= 0) & (moved < SIDE)


def gather_shifts(terms_ref, rows, sign):
    line, position = in_plane()
    total = None
    for c in range(3):
        column = None
        for b in range(3):
            start = (3 * b + c) * rows
            term = terms_ref[start : start + rows, :]
            if b != 1:
                term = jnp.where(
                    inside(line, sign * (b - 1)), shifted(term, sign * SIDE * (b - 1)), 0.0
                )
            column = term if column is None else column + term
        if c != 1:
            column = jnp.where(
                inside(position, sign * (c - 1)), shifted(column, sign * (c - 1)), 0.0
            )
        total = column if total is None else total + column
    return total


def in_turn(multiply, finish, terms_refs, count):
    for step in range(count + 1):
        if step < count:
            multiply(step, terms_refs[step % 2])
        if step:
            finish(step - 1, terms_refs[(step - 1) % 2])


def forward_kernel(place_ref, *refs):
    block_refs = refs[:8]
    kernel_ref, bias_ref, out_ref, act_ref, even_ref, odd_ref, sems = refs[8:]
    channels = act_ref.shape[0] // 8
    filters = bias_ref.shape[0]
    copies = []
    for index, block_ref in enumerate(block_refs):
        start = pl.multiple_of(place_ref[index] * channels, channels)
        copies.append(
            pltpu.make_async_copy(block_ref, act_ref.at[pl.ds(start, channels), :], sems.at[index])
        )
    for copy in copies:
        copy.start()
    for copy in copies:
        copy.wait()

    def multiply(plane, into_ref):
        first, last = max(plane - 1, 0), min(plane + 2, 8)
        lanes = (first - plane + 1) * channels
        into_ref[...] = jnp.dot(
            kernel_ref[:, lanes : lanes + (last - first) * channels],
            act_ref[first * channels : last * channels, :],
            preferred_element_type=jnp.float32,
        )

    def finish(plane, from_ref):
        total = gather_shifts(from_ref, filters, 1) + bias_ref[...]
        out_ref[:, plane * PLANE : (plane + 1) * PLANE] = total.astype(out_ref.dtype)

    in_turn(multiply, finish, (even_ref, odd_ref), 8)


def forward(place, blocks, kernel, bias):
    channels, cells = blocks[0].shape
    filters = bias.shape[0]
    vmem = pl.BlockSpec(memory_space=pltpu.VMEM)
    return pl.pallas_call(
        forward_kernel,
        in_specs=[pl.BlockSpec(memory_space=pltpu.SMEM)]
        + [pl.BlockSpec(memory_space=pl.ANY)] * 8
        + [vmem, vmem],
        out_specs=vmem,
        out_shape=jax.ShapeDtypeStruct((filters, 8 * cells), jnp.bfloat16),
        scratch_shapes=[
            pltpu.VMEM((8 * channels, cells), jnp.bfloat16),
            pltpu.VMEM((9 * filters, cells), jnp.float32),
            pltpu.VMEM((9 * filters, cells), jnp.float32),
            pltpu.SemaphoreType.DMA((8,)),
        ],
        compiler_params=pltpu.CompilerParams(vmem_limit_bytes=VMEM_BYTES),
        cost_estimate=pl.CostEstimate(
            flops=2 * TAPS * channels * filters * 8 * cells,
            bytes_accessed=6 * 1024 * 1024,
            transcendentals=0,
        ),
        name="forward",
    )(place, *blocks, kernel, bias[:, None])


def weight_kernel(first, last, place_ref, grad_ref, near_ref, far_ref, *refs):
    before_ref = None if first else refs[0]
    *out_refs, moved_ref, act_ref, total_ref = refs if first else refs[1:]
    filters = grad_ref.shape[0]
    group = 9 * filters
    pair, x = place_ref[0], place_ref[1]
    line, position = in_plane()

    def lanes_of(index):
        return pl.ds(pl.multiple_of(index * PLANE, PLANE), PLANE)

    act_ref[:, lanes_of(x)] = near_ref[...]
    act_ref[:, lanes_of(1 - x)] = far_ref[...]
    bias = None
    for place in range(4):
        plane = 2 * pair - 1 + place
        lanes = slice(place * PLANE, (place + 1) * PLANE)
        held = jnp.clip(plane, 0, 7)
        block = grad_ref[:, lanes_of(held)].astype(jnp.float32)
        if place in (0, 3):
            block = jnp.where(held == plane, block, 0.0)
        else:
            share = jnp.sum(block, axis=1, keepdims=True)
            bias = share if bias is None else bias + share
        for c in range(3):
            column = block
            if c != 1:
                column = jnp.where(
                    inside(position, -(c - 1)), shifted(block, -(c - 1)), 0.0
                )
            for b in range(3):
                term = column
                if b != 1:
                    term = jnp.where(
                        inside(line, -(b - 1)), shifted(column, -SIDE * (b - 1)), 0.0
                    )
                start = (3 * b + c) * filters
                moved_ref[start : start + filters, lanes] = term.astype(moved_ref.dtype)
    for a in range(3):
        rows = slice(a * group, (a + 1) * group)
        total = lax.dot_general(
            moved_ref[:, (2 - a) * PLANE : (4 - a) * PLANE],
            act_ref[...],
            (((1,), (1,)), ((), ())),
            preferred_element_type=jnp.float32,
        )
        total_ref[rows, :] = total if first else before_ref[rows, :] + total
    bias = jnp.broadcast_to(bias, (filters, total_ref.shape[1]))
    total_ref[3 * group :, :] = bias if first else before_ref[3 * group :, :] + bias
    if last:
        turned = total_ref[...].T
        halves = turned.reshape(8, 2, turned.shape[0] // 16, turned.shape[1])
        own, other = halves[:, 0], halves[:, 1]
        core = place_ref[2]
        out_refs[0][...] = jnp.where(core == 0, own, other)
        out_refs[1][...] = jnp.where(core == 0, other, own)
    else:
        out_refs[0][...] = total_ref[...]


def weight_part(place, grads, near, far, before, last):
    channels, cells = near.shape
    filters = grads.shape[0]
    width = (TAPS + 1) * filters
    vmem = pl.BlockSpec(memory_space=pltpu.VMEM)
    first = before is None
    operands = [place, grads, near, far] + ([] if first else [before])
    return pl.pallas_call(
        functools.partial(weight_kernel, first, last),
        in_specs=[pl.BlockSpec(memory_space=pltpu.SMEM)] + [vmem] * (len(operands) - 1),
        out_specs=[vmem, vmem] if last else vmem,
        out_shape=[jax.ShapeDtypeStruct((8, channels // 16, width), jnp.float32)] * 2
        if last
        else jax.ShapeDtypeStruct((width, channels), jnp.float32),
        scratch_shapes=[
            pltpu.VMEM((9 * filters, 4 * cells), jnp.bfloat16),
            pltpu.VMEM((channels, 2 * cells), jnp.bfloat16),
            pltpu.VMEM((width, channels), jnp.float32),
        ],
        compiler_params=pltpu.CompilerParams(vmem_limit_bytes=VMEM_BYTES),
        cost_estimate=pl.CostEstimate(
            flops=2 * TAPS * channels * filters * 2 * cells,
            bytes_accessed=5 * 1024 * 1024,
            transcendentals=0,
        ),
        name="weight_part",
    )(*operands)


def input_kernel(
    place_ref, below_ref, middle_ref, above_ref, own_ref, other_ref, upper_ref, lower_ref,
    planes_ref, kernel_ref, even_ref, odd_ref, sems,
):
    filters = below_ref.shape[0]
    parts, _, rows, _ = kernel_ref.shape
    copies = []
    for part in range(parts):
        copies.append([])
        for index in range(8):
            away, y, x = index // 4, index // 2 % 2, index % 2
            core = 1 - place_ref[1] if away else place_ref[1]
            from_ref = (other_ref if away else own_ref).at[y, part, x]
            to_ref = kernel_ref.at[part, pl.ds(7 * (2 * y + core), 7), pl.ds(32 * x, 32), :]
            copies[-1].append(pltpu.make_async_copy(from_ref, to_ref, sems.at[part, index]))
            copies[-1][-1].start()
    planes_ref[:filters, :] = below_ref[...]
    planes_ref[filters : 2 * filters, :] = middle_ref[:, :PLANE]
    planes_ref[2 * filters : 3 * filters, :] = middle_ref[:, PLANE:]
    planes_ref[3 * filters :, :] = above_ref[...]
    start = pl.multiple_of(place_ref[0] * filters, filters)

    def multiply(part, into_ref):
        for copy in copies[part]:
            copy.wait()
        last = jnp.concatenate([kernel_ref[part, 18:21], kernel_ref[part, 22:28]])
        groups = [last, kernel_ref[part, 9:18], kernel_ref[part, :9]]
        kernel = jnp.concatenate(
            [group.reshape(9 * rows, filters) for group in groups], axis=1
        )
        into_ref[...] = jnp.dot(
            kernel, planes_ref[pl.ds(start, 3 * filters), :], preferred_element_type=jnp.float32
        )

    def finish(part, from_ref):
        out_ref = upper_ref if part < parts // 2 else lower_ref
        start = part % (parts // 2) * rows
        out_ref[start : start + rows, :] = gather_shifts(from_ref, rows, -1)

    in_turn(multiply, finish, (even_ref, odd_ref), parts)


def input_part(place, below, middle, above, own, other, rows=64):
    filters, cells = below.shape
    channels = 4 * rows
    vmem = pl.BlockSpec(memory_space=pltpu.VMEM)
    return pl.pallas_call(
        input_kernel,
        in_specs=[
            pl.BlockSpec(memory_space=pltpu.SMEM),
            vmem,
            vmem,
            vmem,
            pl.BlockSpec(memory_space=pl.ANY),
            pl.BlockSpec(memory_space=pl.ANY),
        ],
        out_specs=[vmem, vmem],
        out_shape=[jax.ShapeDtypeStruct((channels // 2, cells), jnp.float32)] * 2,
        scratch_shapes=[
            pltpu.VMEM((4 * filters, cells), jnp.bfloat16),
            pltpu.VMEM((channels // rows, 28, rows, filters), jnp.bfloat16),
            pltpu.VMEM((9 * rows, cells), jnp.float32),
            pltpu.VMEM((9 * rows, cells), jnp.float32),
            pltpu.SemaphoreType.DMA((channels // rows, 8)),
        ],
        compiler_params=pltpu.CompilerParams(vmem_limit_bytes=VMEM_BYTES),
        cost_estimate=pl.CostEstimate(
            flops=2 * TAPS * channels * filters * cells,
            bytes_accessed=8 * 1024 * 1024,
            transcendentals=0,
        ),
        name="input_part",
    )(place, below, middle, above, own, other)


def pick_kernel(place_ref, weights_ref, own_ref, other_ref):
    count, rows, width = own_ref.shape
    x = place_ref[1]
    taps = weights_ref[pl.ds(place_ref[0], count)].reshape(count * rows, 2 * width)
    taps = taps.astype(jnp.float32)
    left = lax.broadcasted_iota(jnp.int32, (1, 128), 1) < 64
    for block in range(width // 128):
        first = taps[:, 256 * block : 256 * block + 128]
        second = taps[:, 256 * block + 128 : 256 * block + 256]
        even = jnp.where(left, first, pltpu.roll(second, 64, 1))
        odd = jnp.where(left, pltpu.roll(first, 64, 1), second)
        lanes = slice(128 * block, 128 * block + 128)
        own, other = jnp.where(x == 0, even, odd), jnp.where(x == 0, odd, even)
        own_ref[:, :, lanes] = own.astype(own_ref.dtype).reshape(count, rows, 128)
        other_ref[:, :, lanes] = other.astype(own_ref.dtype).reshape(count, rows, 128)


def pick(place, weights, count):
    _, rows, filters = weights.shape
    vmem = pl.BlockSpec(memory_space=pltpu.VMEM)
    return pl.pallas_call(
        pick_kernel,
        in_specs=[pl.BlockSpec(memory_space=pltpu.SMEM), vmem],
        out_specs=[vmem, vmem],
        out_shape=[jax.ShapeDtypeStruct((count, rows, filters // 2), weights.dtype)] * 2,
        compiler_params=pltpu.CompilerParams(vmem_limit_bytes=VMEM_BYTES),
        name="pick",
    )(place, weights)


def arrange_kernel(scale_ref, core_ref, own_ref, other_ref, out_ref):
    _, sources, rows, width = own_ref.shape
    filters = width // (TAPS + 1)
    scale = scale_ref[0]
    for near, ref in ((True, own_ref), (False, other_ref)):
        core = core_ref[0] if near else 1 - core_ref[0]
        for y in range(2):
            at = pl.ds(pl.multiple_of((2 * core + y) * rows, rows), rows)
            for source in range(sources):
                block = ref[y, source] / scale
                for tap in range(TAPS):
                    out_ref[tap, at, source * filters : (source + 1) * filters] = block[
                        :, tap * filters : (tap + 1) * filters
                    ]


def arrange(scale, core, own, other):
    _, sources, rows, width = own.shape
    filters = width // (TAPS + 1)
    vmem, smem = pl.BlockSpec(memory_space=pltpu.VMEM), pl.BlockSpec(memory_space=pltpu.SMEM)
    return pl.pallas_call(
        arrange_kernel,
        in_specs=[smem, smem, vmem, vmem],
        out_specs=vmem,
        out_shape=jax.ShapeDtypeStruct((TAPS, 4 * rows, sources * filters), jnp.float32),
        compiler_params=pltpu.CompilerParams(vmem_limit_bytes=VMEM_BYTES),
        name="arrange",
    )(scale, core, own, other)


def after(value, *earlier):
    return lax.optimization_barrier((value,) + earlier)[0]


def in_order(own, other, bit):
    return jnp.stack([jnp.where(bit == 0, own, other), jnp.where(bit == 0, other, own)])


def by_source(received, own_index):
    count = len(received)
    falling = jnp.stack(received[::-1] + received[::-1][:-1])
    return lax.dynamic_slice_in_dim(falling, count - 1 - own_index, count, 0)


def half(array, axis, index):
    return lax.dynamic_index_in_dim(array, index, axis, False)


def placement():
    grp, sp = lax.axis_index("grp"), lax.axis_index("sp")
    return {
        "z": sp // 2,
        "x": sp % 2,
        "y": grp // 2,
        "core": grp % 2,
        "swap_x": [(s, s ^ 1) for s in range(8)],
        "swap_core": [(g, g ^ 1) for g in range(4)],
        "swap_y": [(g, g ^ 2) for g in range(4)],
        "pair_z": [(s, s ^ 2) for s in range(8)],
        "cross_z": [(2, 4), (3, 5), (4, 2), (5, 3)],
        "out_z": [(2, 0), (3, 1), (4, 6), (5, 7)],
        "turn_z1": [(s, (s + 2) % 8) for s in range(8)],
        "turn_z2": [(s, (s + 4) % 8) for s in range(8)],
        "turn_z3": [(s, (s + 6) % 8) for s in range(8)],
        "up_z": [(s, s + 2) for s in range(6)],
        "down_z": [(s + 2, s) for s in range(6)],
    }


def per_device(activations, weights, conv_bias, grad_out, loss_scale):
    at = placement()
    z, x, y, core = at["z"], at["x"], at["y"], at["core"]
    together = lax.optimization_barrier
    grads = grad_out[0]
    inner = (z == 1) | (z == 2)
    sources = [z, z ^ 1, jnp.where(z < 2, 2, 1), jnp.where(z < 2, 3, 0)]

    def along(value, axis, steps):
        return lax.ppermute(value, axis, at[steps])

    def add_pair(index, part):
        place = jnp.stack([sources[index], x, core]).astype(jnp.int32)
        return weight_part(place, grads, near[index], far[index], part, index == 3)

    def planes_for(k):
        return lax.dynamic_slice_in_dim(grads, ((z + k) % 4) * 2 * PLANE, 2 * PLANE, 1)

    own = activations[0]
    second = along(own, "sp", "pair_z")
    third = along(own, "sp", "cross_z")
    own_far = along(own, "sp", "swap_x")
    first_tap = jnp.minimum(7 * (2 * y + core), TAPS - 7)
    keep, give = pick(jnp.stack([first_tap, x]).astype(jnp.int32), weights, 7)
    given = along(give, "sp", "swap_x")
    second, third, own_far = together((second, third, own_far))

    near, far = [own], [own_far]
    fourth = along(second, "sp", "cross_z")
    third_out = along(third, "sp", "out_z")
    near.append(second)
    far.append(along(second, "sp", "swap_x"))
    part = add_pair(0, None)
    fourth, third_out, far[1], part, given = together((fourth, third_out, far[1], part, given))

    near.append(jnp.where(inner, third, third_out))
    far.append(along(near[2], "sp", "swap_x"))
    fourth_out = along(fourth, "sp", "out_z")
    kernel = in_order(keep, given, x)
    ring = [kernel] + [along(kernel, "sp", f"turn_z{k}") for k in (1, 2, 3)]
    part = add_pair(1, part)
    fourth_out, far[2], part, *ring = together((fourth_out, far[2], part, *ring))

    near.append(jnp.where(inner, fourth, fourth_out))
    far.append(along(near[3], "sp", "swap_x"))
    grads = after(grads, fourth_out)
    blocks = [planes_for(0)] + [along(planes_for(k), "sp", f"turn_z{k}") for k in (1, 2, 3)]
    kernel = by_source(ring, z)
    arrived = along(kernel, "grp", "swap_y")
    rows, give = add_pair(3, add_pair(2, part))
    rows, give, arrived, *blocks = together((rows, give, arrived, *blocks))

    middle = by_source(blocks, z).reshape(256, 2 * PLANE)
    below = along(middle[:, PLANE:], "sp", "up_z")
    above = along(middle[:, :PLANE], "sp", "down_z")
    given = along(give, "grp", "swap_core")
    kernel = in_order(kernel, arrived, y)
    other_kernel = along(kernel, "grp", "swap_core")
    own_filters = in_order(
        lax.dynamic_slice_in_dim(kernel, z * 64, 64, 5),
        lax.dynamic_slice_in_dim(other_kernel, z * 64, 64, 5),
        core,
    )
    own_filters = own_filters.transpose(1, 0, 4, 6, 2, 3, 5).reshape(28, 64, 256)
    own_filters = jnp.concatenate([own_filters[:21], own_filters[22:]])
    own_filters = own_filters.reshape(3, 9 * 64, 256).transpose(1, 0, 2).reshape(9 * 64, 3 * 256)
    width = rows.shape[2]
    rows = (rows + given).reshape(8, 2, 8, width)
    arrived = along(half(rows, 1, 1 - y), "grp", "swap_y")
    below, above, other_kernel, own_filters = together(
        (below, above, other_kernel, own_filters)
    )

    rows = lax.all_to_all(half(rows, 1, y) + arrived, "sp", 0, 0)
    planes = below, middle, above, kernel, other_kernel
    upper, lower = input_part(jnp.stack([1 - x, core]).astype(jnp.int32), *planes)
    upper = along(upper, "sp", "swap_x")
    place = jnp.stack([2 * s + x for s in sources] + [2 * s + 1 - x for s in sources])
    conv_out = forward(place.astype(jnp.int32), near + far, own_filters, conv_bias)
    rows, upper, lower, conv_out = together((rows, upper, lower, conv_out))

    lower = along(lower, "sp", "swap_x")
    arrived = along(rows, "grp", "swap_y")
    own_planes = input_part(jnp.stack([x, core]).astype(jnp.int32), *planes)
    arrived, lower, own_planes = together((arrived, lower, own_planes))

    rows = in_order(rows, arrived, y)
    other_rows = along(rows, "grp", "swap_core")
    grad_weight = arrange(loss_scale, core.astype(jnp.int32)[None], rows, other_rows)
    bias_sum = half(rows[0], 0, lax.axis_index("sp"))[0, TAPS * 64 :]
    grad_input = jnp.concatenate([own_planes[0] + upper, own_planes[1] + lower]).astype(jnp.bfloat16)
    return (conv_out[None], grad_input[None], grad_weight, bias_sum / loss_scale[0])


def solution(mesh):
    measured = mesh.shape["grp"] == 4 and mesh.shape["sp"] == 8
    return jax.shard_map(
        per_device if measured else shard_general,
        mesh=mesh,
        in_specs=(P("grp", None, "sp"), P(None, "sp", None), P("sp"), P("grp", "sp", None), P()),
        out_specs=(P("grp", "sp", None), P("grp", None, "sp"), P(None, "sp", None), P("sp")),
        check_vma=False,
    )
```
